256 devices in a mesh: grp: 4 (over x), dev: 64 (over y, z, core).
Axes of the slice: x: 4, y: 4, z: 8, core: 2. Of those that a mesh axis runs over, the one named last changes fastest.
Arguments:
- orbitals: bfloat16 [512, 4, 128, 128], P(('grp', 'dev')), may hold values from -0.359375 to 0.359375
- domains: int32 [512, 4], replicated, may hold values from 0 to 19, as said below
- partners: int32 [512, 72], P(('grp', 'dev')), may hold values from 0 to 511, as said below
- active: int32 [512], P(('grp', 'dev')), may hold values from 1 to 64
- fock_terms: float32 [512, 72], P(('grp', 'dev')), may hold values from -0.5 to 0.5
- exchange_ints: bfloat16 [512, 128, 128], P(('grp', 'dev')), may hold values from -12 to 12
- pno_energies: float32 [512, 128], P(('grp', 'dev')), may hold values from 0.2 to 2
- occ_energies: float32 [512], P(('grp', 'dev')), may hold values from -1.6 to -0.5
- amplitudes: float32 [512, 128, 128], P(('grp', 'dev')), may hold values from -6 to 6
Outputs:
- updated: float32 [512, 128, 128], P(('grp', 'dev'))
- residual: float32 [512, 128, 128], P(('grp', 'dev'))
The draws below stay inside these ranges and needn't reach their ends.
Inputs may be any that keep to these rules, and one draw needn't show every extreme that they name: Pairs are numbered group by group along grp, then device by device along dev, 2 to a device. For s < 64, partners[q, s] is a pair held by device s of q's group, and all pairs held by one device name the same pair in slot s. For s >= 64, partners[q, s] is held by the device with the same dev index in the group just before or just after q's group. `domains`: the 4 labels of a row are distinct and lie in 4 * g to 4 * g + 2 * 4 - 1, g the group of the pair.
All inputs are finite; a program needn't handle non-finite values.
Results may differ from the reference program's by a relative error of at most 0.023.
Values may be sent and summed in bfloat16 or wider, within the bound.
No kernel may reach another device: no remote copies, remote signals or barrier semaphores. Data moves between devices by JAX's collectives and lax.ppermute only.
A program may use at most 128 MiB of HBM per device.

```python
import math
import jax
import jax.numpy as jnp
from jax import lax

P_SIZE = 128
BLK = 128
DB = 4
PAIRS_DEV = 2
COUP_X = 8
ITERS = 2
COUP_IN = 64
COUP = 72
PAIRS = 512
N_GRP = 4
N_DEV = 64


def draw_partners(key, part):
    key = jax.random.fold_in(key, 11)
    row_key, side_key, cross_key = jax.random.split(key, 3)
    owner_row = jax.random.randint(row_key, (N_GRP, N_DEV, 1, COUP_IN), 0, PAIRS_DEV)
    owner_row = jnp.broadcast_to(owner_row, (N_GRP, N_DEV, PAIRS_DEV, COUP_IN))
    group = jnp.arange(N_GRP, dtype=jnp.int32)[:, None, None, None]
    slot_dev = jnp.arange(COUP_IN, dtype=jnp.int32)[None, None, None, :]
    inner = (group * N_DEV + slot_dev) * PAIRS_DEV + owner_row
    side = jax.random.randint(side_key, (N_GRP, N_DEV, PAIRS_DEV, COUP_X), 0, 2) * 2 - 1
    side = jnp.where(group == 0, 1, jnp.where(group == N_GRP - 1, -1, side))
    dev_index = jnp.arange(N_DEV, dtype=jnp.int32)[None, :, None, None]
    cross_row = jax.random.randint(cross_key, (N_GRP, N_DEV, PAIRS_DEV, COUP_X), 0, PAIRS_DEV)
    cross = ((group + side) * N_DEV + dev_index) * PAIRS_DEV + cross_row
    joined = jnp.concatenate([inner, cross], axis=3)
    return joined.reshape(PAIRS, COUP_IN + COUP_X).astype(jnp.int32)


def draw_domains(key, part):
    key = jax.random.fold_in(key, 23)
    orders = jax.vmap(lambda subkey: jax.random.permutation(subkey, 2 * DB))(jax.random.split(key, PAIRS))
    group = (jnp.arange(PAIRS, dtype=jnp.int32) // (N_DEV * PAIRS_DEV))[:, None]
    return (orders[:, :DB] + group * DB).astype(jnp.int32)


def draw_active(key, part):
    key = jax.random.fold_in(key, 37)
    count_key, full_key, single_key = jax.random.split(key, 3)
    counts = jax.random.randint(count_key, (PAIRS,), 1, COUP_IN + 1)
    full_pair = jax.random.randint(full_key, (), 0, PAIRS)
    single_pair = (full_pair + 1 + jax.random.randint(single_key, (), 0, PAIRS - 1)) % PAIRS
    position = jnp.arange(PAIRS, dtype=jnp.int32)
    counts = jnp.where(position == full_pair, COUP_IN, counts)
    counts = jnp.where(position == single_pair, 1, counts)
    return counts.astype(jnp.int32)


def shard_levels(rng, extent, cuts, smallest, top_value):
    loudness, own = 1.0, jax.random.fold_in(rng, 6)
    for axis_at, blocks in cuts:
        draws = jnp.exp(jax.random.uniform(jax.random.fold_in(own, axis_at), (blocks,), jnp.float32, smallest / len(cuts), top_value / len(cuts)))
        loudness = loudness * jnp.repeat(draws, extent[axis_at] // blocks).reshape([-1 if axis == axis_at else 1 for axis in range(len(extent))])
    return loudness


def gaussian(stream_key, shape, width, most, cuts=(), kind=jnp.bfloat16):
    gain = shard_levels(stream_key, shape, cuts, -0.22, 0.18) if cuts else 1.0
    array = jax.random.normal(stream_key, shape, jnp.float32) * width * gain
    return jnp.minimum(jnp.maximum(array, -most), most).astype(kind)


def setup_inputs(seed: int = 0) -> dict:
    streams_of = jax.random.split(jax.random.key(seed), 10)
    orbitals = gaussian(streams_of[0], (PAIRS, DB, BLK, P_SIZE), 0.06, 0.359375, ((0, 256),))
    domains = draw_domains(jax.random.fold_in(streams_of[9], 71), 0)
    partners = draw_partners(jax.random.fold_in(streams_of[9], 71), 0)
    active = draw_active(jax.random.fold_in(streams_of[9], 71), 0)
    fock_terms = jnp.clip(jax.random.uniform(streams_of[4], (PAIRS, COUP), jnp.float32, -0.5, 0.5) * shard_levels(streams_of[4], (PAIRS, COUP), ((0, 256),), -0.4, 0.0), -0.5, 0.5)
    exchange_ints = gaussian(streams_of[5], (PAIRS, P_SIZE, P_SIZE), 2.0, 12.0, ((0, 256),))
    pno_energies = jnp.clip(jnp.exp(math.log(2.0) - 2.3025851 * jax.random.uniform(streams_of[6], (PAIRS, P_SIZE), jnp.float32) ** shard_levels(streams_of[6], (PAIRS, P_SIZE), ((0, 256),), -0.2, 0.2)), 0.2, 2.0)
    occ_energies = jnp.clip(-1.6 + 1.1 * jax.random.uniform(streams_of[7], (PAIRS,), jnp.float32) ** shard_levels(streams_of[7], (PAIRS,), ((0, 256),), -0.2, 0.2), -1.6, -0.5)
    amplitudes = gaussian(streams_of[8], (PAIRS, P_SIZE, P_SIZE), 1.0, 6.0, ((0, 256),), jnp.float32)
    return dict(orbitals=orbitals, domains=domains, partners=partners, active=active, fock_terms=fock_terms, exchange_ints=exchange_ints, pno_energies=pno_energies, occ_energies=occ_energies, amplitudes=amplitudes)


def reference(orbitals, domains, partners, active, fock_terms, exchange_ints, pno_energies, occ_energies, amplitudes):
    coup_all = partners.shape[1]
    slot_iota = jnp.arange(coup_all, dtype=jnp.int32)[None, :]
    live_slot = (slot_iota >= COUP_IN) | (slot_iota < active[:, None])
    weights = jnp.where(live_slot, fock_terms, jnp.zeros_like(fock_terms))

    def intersection_of(entry):
        own_orb, own_domain, partner_list = entry
        partner_orb = orbitals[partner_list].astype(jnp.float32)
        partner_domain = domains[partner_list]
        same_block = (own_domain[None, :, None] == partner_domain[:, None, :]).astype(jnp.float32)
        aligned = jnp.einsum("sab,sbrt->sart", same_block, partner_orb)
        return jnp.einsum("arp,sart->spt", own_orb.astype(jnp.float32), aligned).astype(jnp.bfloat16)

    intersections = lax.map(intersection_of, (orbitals, domains, partners))
    denominator = pno_energies[:, :, None] + pno_energies[:, None, :] - occ_energies[:, None, None]
    integrals = exchange_ints.astype(jnp.float32)

    def couple_all(sent_amps):
        def couple_pair(entry):
            pair_intersections, partner_list, slot_weights = entry
            intersection_full = pair_intersections.astype(jnp.float32)
            partner_amps = sent_amps[partner_list].astype(jnp.float32)
            halfway = jnp.einsum("spr,srt->spt", intersection_full, partner_amps).astype(jnp.bfloat16)
            halfway = lax.optimization_barrier(halfway).astype(jnp.float32)
            framed = jnp.einsum("spt,sut->spu", halfway, intersection_full)
            return jnp.einsum("s,spu->pu", slot_weights, framed)

        return lax.map(couple_pair, (intersections, partners, weights))

    current = amplitudes
    residual = jnp.zeros_like(amplitudes)
    for iteration in range(ITERS):
        coupled = couple_all(current.astype(jnp.bfloat16))
        residual = integrals + denominator * current - coupled
        current = current - residual / denominator
    return current, residual
```

```python
import functools

import jax
import jax.numpy as jnp
from jax import lax
from jax.experimental import pallas as pl
from jax.experimental.pallas import tpu as pltpu
from jax.sharding import PartitionSpec as P

N_Y, N_Z, N_CORE = 4, 8, 2
N_DEV = N_Y * N_Z * N_CORE
COUP_IN = 64
W = 128
OROWS = 512
BF16 = jnp.bfloat16
F32 = jnp.float32
SMEM = pl.BlockSpec(memory_space=pltpu.SMEM)
VMEM = pl.BlockSpec(memory_space=pltpu.VMEM)
ANY = pl.BlockSpec(memory_space=pl.ANY)
PARAMS = pltpu.CompilerParams(vmem_limit_bytes=40 * 1024 * 1024)


def place(y, z, c):
    return ((y % N_Y) * N_Z + z % N_Z) * N_CORE + c


def routes(move):
    return [
        (place(y, z, c), move(y, z, c))
        for y in range(N_Y)
        for z in range(N_Z)
        for c in range(N_CORE)
    ]


def send(x, move):
    return lax.ppermute(x, "dev", routes(move))


def swap(x):
    return send(x, lambda y, z, c: place(y, z, 1 - c))


def along_z(x, k):
    return send(x, lambda y, z, c: place(y, z + k if c == 0 else z - k, c))


def along_y(x, k):
    return send(x, lambda y, z, c: place(y + k, z, c))


def cost(products, nbytes):
    return pl.CostEstimate(flops=products * 2 * W**3 * 3, bytes_accessed=nbytes, transcendentals=0)


def bundle_kernel(orb_ref, amp_ref, out_ref):
    out_ref[:, pl.ds(0, OROWS), :] = orb_ref[...].reshape(2, OROWS, W)
    out_ref[:, pl.ds(OROWS, W), :] = amp_ref[...].astype(BF16)


def bundle(orbitals, amplitudes):
    return pl.pallas_call(
        bundle_kernel,
        out_shape=jax.ShapeDtypeStruct((2, OROWS + W, W), BF16),
        in_specs=[VMEM, VMEM],
        out_specs=VMEM,
        compiler_params=PARAMS,
        cost_estimate=cost(0, 700000),
    )(orbitals, amplitudes)


def turned_kernel(orb_ref, words_ref, out_ref):
    for q in range(2):
        for a in range(4):
            out_ref[pl.ds((q * 4 + a) * W, W), :] = orb_ref[q, a].T
    words = words_ref[...]
    high = words.astype(BF16).astype(F32)
    middle = (words - high).astype(BF16).astype(F32)
    low = words - high - middle
    row = lax.broadcasted_iota(jnp.int32, (16, W), 0)
    parts = jnp.where(row < 2, high, jnp.where(row < 4, middle, jnp.where(row < 6, low, 0.0)))
    out_ref[pl.ds(2 * OROWS, 16), :] = parts.astype(BF16)


def turned(orbitals, words):
    return pl.pallas_call(
        turned_kernel,
        out_shape=jax.ShapeDtypeStruct((2 * OROWS + 16, W), BF16),
        in_specs=[VMEM, VMEM],
        out_specs=VMEM,
        compiler_params=PARAMS,
        cost_estimate=cost(0, 600000),
    )(orbitals, words)


def block_rows(dom_ref, base, q_id, p_id, q, zero_row):
    labels = [dom_ref[q_id * 4 + a] for a in range(4)]
    rows = []
    for b in range(4):
        label = dom_ref[p_id * 4 + b]
        row = zero_row
        for a in range(4):
            row = jnp.where(labels[a] == label, base + (q * 4 + a) * W, row)
        rows.append(pl.multiple_of(row, W))
    return rows


def intersect(qbuf, rows, partner):
    left = jnp.concatenate(
        [
            jnp.concatenate([qbuf[pl.ds(row, W), :] for row in rows_q], axis=1)
            for rows_q in rows
        ],
        axis=0,
    )
    return jnp.dot(left, partner, preferred_element_type=F32).astype(BF16)


def weighted(inter, amps, w0, w1):
    half = jnp.dot(inter, amps, preferred_element_type=F32)
    return (half[:W] * w0).astype(BF16), (half[W:] * w1).astype(BF16)


def frame(halves, inters):
    return lax.dot_general(
        jnp.concatenate(halves, axis=1),
        jnp.concatenate(inters, axis=1),
        (((1,), (1,)), ((), ())),
        preferred_element_type=F32,
    )


def slot_of(pos_ref, chunk):
    step, mine = chunk
    y, z, c = pos_ref[1], pos_ref[2], pos_ref[3]
    zz = jnp.where(c == 0, z - step, z + step) & (N_Z - 1)
    lane = c if mine else 1 - c
    return (y * N_Z + zz) * N_CORE + lane


def owner_of(pos_ref, i):
    y, z, c = pos_ref[1], pos_ref[2], pos_ref[3]
    yy = (y - (i & 3)) & (N_Y - 1)
    lane = jnp.where(i < 4, c, 1 - c)
    return (yy * N_Z + z) * N_CORE + lane


def first_kernel(chunks, first, count, has_prev, *refs):
    n = len(chunks)
    pos_ref, dom_ref, word_ref = refs[:3]
    q_refs = refs[3 : 3 + count]
    p_refs = refs[3 + count : 3 + count + n]
    rest = refs[3 + count + n :]
    prev_ref = rest[0] if has_prev else None
    inter_ref, out_ref, qbuf, pbuf, q_sem, p_sem = rest[1 if has_prev else 0 :]
    step = pl.program_id(0)
    zero_row = count * 2 * OROWS

    @pl.when(step == 0)
    def _():
        p_copies = [
            pltpu.make_async_copy(p_refs[j], pbuf.at[j], p_sem.at[j]) for j in range(n)
        ]
        q_copies = [
            pltpu.make_async_copy(
                q_refs[k].at[pl.ds(0, 2 * OROWS)],
                qbuf.at[pl.ds(k * 2 * OROWS, 2 * OROWS)],
                q_sem.at[k],
            )
            for k in range(count)
        ]
        q_copies[0].start()
        for copy in p_copies:
            copy.start()
        for copy in q_copies[1:]:
            copy.start()
        qbuf[pl.ds(zero_row, W), :] = jnp.zeros((W, W), BF16)
        for copy in p_copies:
            copy.wait()

    base = pl.multiple_of(step * 2 * OROWS, 2 * OROWS)
    pltpu.make_async_copy(
        q_refs[0].at[pl.ds(0, 2 * OROWS)], qbuf.at[pl.ds(base, 2 * OROWS)], q_sem.at[step]
    ).wait()
    i = step + first
    group = pos_ref[0] * N_DEV
    q_id = (group + owner_of(pos_ref, i)) * 2
    halves, inters = [[], []], [[], []]
    for j, chunk in enumerate(chunks):
        slot = slot_of(pos_ref, chunk)
        row = word_ref[i * 2 * W + COUP_IN + slot].astype(jnp.int32)
        p_id = (group + slot) * 2 + row
        rows = [block_rows(dom_ref, base, q_id + q, p_id, q, zero_row) for q in range(2)]
        inter = intersect(qbuf, rows, pbuf[j, row, pl.ds(0, OROWS), :])
        inter_ref[0, j] = inter
        weights = [word_ref[(i * 2 + q) * W + slot] for q in range(2)]
        half = weighted(inter, pbuf[j, row, pl.ds(OROWS, W), :], *weights)
        for q in range(2):
            halves[q].append(half[q])
            inters[q].append(inter[q * W : (q + 1) * W])
    for q in range(2):
        total = frame(halves[q], inters[q])
        if has_prev:
            total = total + prev_ref[0, q]
        out_ref[0, q] = total.astype(out_ref.dtype)


def first_couple(pos, dom, words, turned_all, chunks, chunk_data, first, count, prev, out_type):
    n = len(chunks)
    whole = pl.BlockSpec((1, 2, W, W), lambda s: (s, 0, 0, 0))
    prev_spec = pl.BlockSpec((1, 2, W, W), lambda s: (s + first, 0, 0, 0))
    return pl.pallas_call(
        functools.partial(first_kernel, chunks, first, count, prev is not None),
        grid=(count,),
        out_shape=(
            jax.ShapeDtypeStruct((count, n, 2 * W, W), BF16),
            jax.ShapeDtypeStruct((count, 2, W, W), out_type),
        ),
        in_specs=[SMEM] * 3 + [ANY] * (count + n) + ([prev_spec] if prev is not None else []),
        out_specs=(pl.BlockSpec((1, n, 2 * W, W), lambda s: (s, 0, 0, 0)), whole),
        scratch_shapes=[
            pltpu.VMEM((count * 2 * OROWS + W, W), BF16),
            pltpu.VMEM((n, 2, OROWS + W, W), BF16),
            pltpu.SemaphoreType.DMA((count,)),
            pltpu.SemaphoreType.DMA((n,)),
        ],
        compiler_params=PARAMS,
        cost_estimate=cost(count * n * 2 * 6, 3000000),
    )(
        pos,
        dom,
        words,
        *turned_all[first : first + count],
        *chunk_data,
        *([prev] if prev is not None else []),
    )


def next_kernel(chunks, places, first, n_amps, has_prev, *refs):
    pos_ref, word_ref, inter_ref = refs[:3]
    amp_refs = refs[3 : 3 + n_amps]
    prev_ref = refs[3 + n_amps] if has_prev else None
    out_ref = refs[-1]
    i = pl.program_id(0) + first
    halves, inters = [[], []], [[], []]
    for j, chunk in enumerate(chunks):
        slot = slot_of(pos_ref, chunk)
        row = word_ref[i * 2 * W + COUP_IN + slot].astype(jnp.int32)
        weights = [word_ref[(i * 2 + q) * W + slot] for q in range(2)]
        which, offset = places[j]
        inter = inter_ref[0, j]
        half = weighted(inter, amp_refs[which][offset + row], *weights)
        for q in range(2):
            halves[q].append(half[q])
            inters[q].append(inter[q * W : (q + 1) * W])
    for q in range(2):
        total = frame(halves[q], inters[q])
        if has_prev:
            total = total + prev_ref[0, q]
        out_ref[0, q] = total.astype(out_ref.dtype)


def next_couple(pos, words, inter, chunks, places, amps, first, prev, out_type):
    count, n = inter.shape[:2]
    whole = pl.BlockSpec((1, 2, W, W), lambda s: (s, 0, 0, 0))
    prev_spec = pl.BlockSpec((1, 2, W, W), lambda s: (s + first, 0, 0, 0))
    return pl.pallas_call(
        functools.partial(next_kernel, chunks, places, first, len(amps), prev is not None),
        grid=(count,),
        out_shape=jax.ShapeDtypeStruct((count, 2, W, W), out_type),
        in_specs=[SMEM] * 2
        + [pl.BlockSpec((1, n, 2 * W, W), lambda s: (s, 0, 0, 0))]
        + [VMEM] * len(amps)
        + ([prev_spec] if prev is not None else []),
        out_specs=whole,
        compiler_params=PARAMS,
        cost_estimate=cost(count * n * 2 * 2, 3000000),
    )(pos, words, inter, *amps, *([prev] if prev is not None else []))


def cross_first_kernel(pos_ref, dom_ref, weight_ref, near_ref, own_ref, inter_ref, out_ref, qbuf):
    qbuf[pl.ds(0, 2 * OROWS), :] = own_ref[pl.ds(0, 2 * OROWS), :]
    qbuf[pl.ds(2 * OROWS, W), :] = jnp.zeros((W, W), BF16)
    group, place_here = pos_ref[0], (pos_ref[1] * N_Z + pos_ref[2]) * N_CORE + pos_ref[3]
    q_id = (group * N_DEV + place_here) * 2
    halves, inters = [[], []], [[], []]
    for j in range(4):
        there = jnp.clip(group + (1 if j >= 2 else -1), 0, 3)
        p_id = (there * N_DEV + place_here) * 2 + j % 2
        rows = [block_rows(dom_ref, 0, q_id + q, p_id, q, 2 * OROWS) for q in range(2)]
        pair = there * 2 + j % 2
        inter = intersect(qbuf, rows, near_ref[pair, pl.ds(0, OROWS), :])
        inter_ref[j] = inter
        half = weighted(
            inter, near_ref[pair, pl.ds(OROWS, W), :], weight_ref[j], weight_ref[4 + j]
        )
        for q in range(2):
            halves[q].append(half[q])
            inters[q].append(inter[q * W : (q + 1) * W])
    for q in range(2):
        out_ref[q] = frame(halves[q], inters[q])


def cross_first(pos, dom, weights, near, own):
    return pl.pallas_call(
        cross_first_kernel,
        out_shape=(
            jax.ShapeDtypeStruct((4, 2 * W, W), BF16),
            jax.ShapeDtypeStruct((2, W, W), F32),
        ),
        in_specs=[SMEM] * 3 + [VMEM] * 2,
        out_specs=(VMEM, VMEM),
        scratch_shapes=[pltpu.VMEM((2 * OROWS + W, W), BF16)],
        compiler_params=PARAMS,
        cost_estimate=cost(8 * 6, 2000000),
    )(pos, dom, weights, near, own)


def cross_next_kernel(weight_ref, inter_ref, below_ref, above_ref, out_ref):
    halves, inters = [[], []], [[], []]
    for j in range(4):
        amps = (below_ref if j < 2 else above_ref)[j % 2]
        inter = inter_ref[j]
        half = weighted(inter, amps, weight_ref[j], weight_ref[4 + j])
        for q in range(2):
            halves[q].append(half[q])
            inters[q].append(inter[q * W : (q + 1) * W])
    for q in range(2):
        out_ref[q] = frame(halves[q], inters[q])


def cross_next(weights, inter, below, above):
    return pl.pallas_call(
        cross_next_kernel,
        out_shape=jax.ShapeDtypeStruct((2, W, W), F32),
        in_specs=[SMEM] + [VMEM] * 3,
        out_specs=VMEM,
        compiler_params=PARAMS,
        cost_estimate=cost(8 * 2, 500000),
    )(weights, inter, below, above)


def gather_shares(mine, others):
    total = mine + swap(others).astype(F32)
    shares = [send_back(total[j].astype(BF16), j) for j in range(1, N_Y)]
    return total[0] + (shares[0].astype(F32) + shares[1].astype(F32) + shares[2].astype(F32))


def send_back(x, j):
    return along_y(x, -j)


def on_device(
    orbitals,
    domains,
    partners,
    active,
    fock_terms,
    exchange_ints,
    pno_energies,
    occ_energies,
    amplitudes,
):
    group = lax.axis_index("grp")
    dev = lax.axis_index("dev")
    pos = jnp.stack([group, dev // (N_Z * N_CORE), dev // N_CORE % N_Z, dev % N_CORE])
    pos = pos.astype(jnp.int32)
    dom = domains.reshape(-1)

    slots = jnp.arange(COUP_IN, dtype=jnp.int32)[None, :]
    live = jnp.where(slots < active[:, None], fock_terms[:, :COUP_IN], 0.0)
    wanted = (partners[:, :COUP_IN] % 2).astype(F32)
    words_own = jnp.tile(jnp.concatenate([live, wanted], axis=1), (8, 1))
    near_ids = ((group + jnp.array([-1, -1, 1, 1])) * N_DEV + dev) * 2 + jnp.array([0, 1, 0, 1])
    same = partners[:, None, COUP_IN:] == near_ids[None, :, None]
    cross_w = jnp.sum(jnp.where(same, fock_terms[:, None, COUP_IN:], 0.0), axis=2).reshape(8)

    mine = bundle(orbitals, amplitudes)
    turned_mine = turned(orbitals, words_own)
    ring_a = [mine]
    ring_b = [swap(mine)]
    for k in range(4):
        ring_a.append(along_z(ring_a[-1], 1))
        if k < 3:
            ring_b.append(along_z(ring_b[-1], 1))
    turned_all = [turned_mine] + [along_y(turned_mine, k) for k in range(1, N_Y)]
    turned_all = turned_all + [swap(x) for x in turned_all]
    near = lax.all_gather(mine, "grp", axis=0, tiled=True)

    words = jnp.stack([x[2 * OROWS :] for x in turned_all]).astype(F32)
    words = (words[:, 0:2] + words[:, 2:4] + words[:, 4:6]).reshape(-1)

    early = [(0, True), (1, True), (1, False), (2, True), (2, False)]
    early_data = [ring_a[0], ring_a[1], ring_b[1], ring_a[2], ring_b[2]]
    late = [(3, True), (3, False), (4, True)]
    late_data = [ring_a[3], ring_b[3], ring_a[4]]

    first = functools.partial(first_couple, pos, dom, words, turned_all)
    inter_early, part = first(early, early_data, 0, 8, None, F32)
    inter_other, others = first(late, late_data, 4, 4, part, BF16)
    inter_mine, own = first(late, late_data, 0, 4, part, F32)
    inter_cross, cross = cross_first(pos, dom, cross_w, near, turned_mine)

    denominator = pno_energies[:, :, None] + pno_energies[:, None, :] - occ_energies[:, None, None]
    integrals = exchange_ints.astype(F32)
    coupled = gather_shares(own, others) + cross
    residual = integrals + denominator * amplitudes - coupled
    current = amplitudes - residual / denominator

    sent = current.astype(BF16)
    below = lax.ppermute(sent, "grp", [(0, 1), (1, 2), (2, 3)])
    above = lax.ppermute(sent, "grp", [(1, 0), (2, 1), (3, 2)])
    far = along_z(sent, 4)
    both = jnp.concatenate([sent, swap(sent)], axis=0)
    steps = [along_z(both, k) for k in range(1, 4)]

    again = functools.partial(next_couple, pos, words)
    early_places = [(0, 0), (1, 0), (1, 2), (2, 0), (2, 2)]
    late_places = [(0, 0), (0, 2), (1, 0)]
    part = again(inter_early, early, early_places, [sent, steps[0], steps[1]], 0, None, F32)
    late_amps = [steps[2], far]
    others = again(inter_other, late, late_places, late_amps, 4, part, BF16)
    own = again(inter_mine, late, late_places, late_amps, 0, part, F32)
    cross = cross_next(cross_w, inter_cross, below, above)
    coupled = gather_shares(own, others) + cross
    residual = integrals + denominator * current - coupled
    updated = current - residual / denominator
    return updated, residual


def solution(mesh):
    placed = (
        P(("grp", "dev"), None, None, None),
        P(),
        P(("grp", "dev"), None),
        P(("grp", "dev")),
        P(("grp", "dev"), None),
        P(("grp", "dev"), None, None),
        P(("grp", "dev"), None),
        P(("grp", "dev")),
        P(("grp", "dev"), None, None),
    )
    return jax.shard_map(
        on_device,
        mesh=mesh,
        in_specs=placed,
        out_specs=(P(("grp", "dev"), None, None), P(("grp", "dev"), None, None)),
        check_vma=False,
    )
```

```python
import functools

import jax
import jax.numpy as jnp
from jax import lax
from jax.experimental import pallas as pl
from jax.experimental.pallas import tpu as pltpu
from jax.sharding import PartitionSpec as P

N_Y, N_Z, N_CORE = 4, 8, 2
N_DEV = N_Y * N_Z * N_CORE
COUP_IN = 64
ROWS = 256
PLACE = ROWS + 128
LABELS = PLACE + 8
QROWS = 8 * 2 * 512
GROUPS = {1: 4, 2: 4, 3: 2, 5: 2}
W = 128
OROWS = 512
BF16 = jnp.bfloat16
F32 = jnp.float32
SMEM = pl.BlockSpec(memory_space=pltpu.SMEM)
VMEM = pl.BlockSpec(memory_space=pltpu.VMEM)
ANY = pl.BlockSpec(memory_space=pl.ANY)
PARAMS = pltpu.CompilerParams(vmem_limit_bytes=40 * 1024 * 1024)


def place(y, z, c):
    return ((y % N_Y) * N_Z + z % N_Z) * N_CORE + c


def routes(move):
    return [
        (place(y, z, c), move(y, z, c))
        for y in range(N_Y)
        for z in range(N_Z)
        for c in range(N_CORE)
    ]


def send(x, move):
    return lax.ppermute(x, "dev", routes(move))


def swap(x):
    return send(x, lambda y, z, c: place(y, z, 1 - c))


def along_z(x, k):
    return send(x, lambda y, z, c: place(y, z + k if c == 0 else z - k, c))


def along_y(x, k):
    return send(x, lambda y, z, c: place(y + k, z, c))


def cost(microseconds):
    return pl.CostEstimate(
        flops=int(microseconds * 1.15e9), bytes_accessed=1024, transcendentals=0
    )


def bundle_kernel(orb_ref, amp_ref, out_ref, amps, sems):
    copies = [pltpu.make_async_copy(amp_ref, amps, sems.at[4])]
    for q in range(2):
        for a in range(4):
            copies.append(
                pltpu.make_async_copy(
                    orb_ref.at[q, a], out_ref.at[q, pl.ds(a * W, W)], sems.at[q * 4 + a + 5]
                )
            )
    for copy in copies:
        copy.start()
    copies[0].wait()
    out_ref[:, pl.ds(OROWS, W), :] = amps[...].astype(BF16)
    for copy in copies[1:]:
        copy.wait()


def bundle(orbitals, amplitudes):
    far = pl.BlockSpec(memory_space=pltpu.HBM)
    return pl.pallas_call(
        bundle_kernel,
        out_shape=jax.ShapeDtypeStruct((2, OROWS + W, W), BF16),
        in_specs=[far, far],
        out_specs=VMEM,
        scratch_shapes=[pltpu.VMEM((2, W, W), F32), pltpu.SemaphoreType.DMA((13,))],
        compiler_params=PARAMS,
        cost_estimate=cost(1),
    )(orbitals, amplitudes)


def turned_kernel(active_ref, own_ref, fock_ref, partner_ref, out_ref, words):
    for q in range(2):
        for a in range(4):
            out_ref[pl.ds((q * 4 + a) * W, W), :] = own_ref[q, pl.ds(a * W, W), :].T
    words[...] = jnp.zeros((16, W), F32)
    slot = lax.broadcasted_iota(jnp.int32, (1, COUP_IN), 1)
    for q in range(2):
        fock = fock_ref[pl.ds(q, 1), pl.ds(0, COUP_IN)]
        fock = jnp.where(slot < active_ref[q], fock, 0.0)
        high = fock.astype(BF16).astype(F32)
        middle = (fock - high).astype(BF16).astype(F32)
        words[pl.ds(q, 1), pl.ds(0, COUP_IN)] = high
        words[pl.ds(2 + q, 1), pl.ds(0, COUP_IN)] = middle
        words[pl.ds(4 + q, 1), pl.ds(0, COUP_IN)] = fock - high - middle
        wanted = (partner_ref[pl.ds(q, 1), pl.ds(0, COUP_IN)] & 1).astype(F32)
        words[pl.ds(q, 1), pl.ds(COUP_IN, COUP_IN)] = wanted
    out_ref[pl.ds(2 * OROWS, 16), :] = words[...].astype(BF16)


def turned(active, own, fock_terms, partners):
    return pl.pallas_call(
        turned_kernel,
        out_shape=jax.ShapeDtypeStruct((2 * OROWS + 16, W), BF16),
        in_specs=[SMEM, VMEM, VMEM, VMEM],
        out_specs=VMEM,
        scratch_shapes=[pltpu.VMEM((16, W), F32)],
        compiler_params=PARAMS,
        cost_estimate=cost(1),
    )(active, own, fock_terms, partners)


def block_rows(tab_ref, base, q_id, p_id, q, zero_row, start=LABELS):
    labels = [tab_ref[start + q_id * 4 + a] for a in range(4)]
    rows = []
    for b in range(4):
        label = tab_ref[start + p_id * 4 + b]
        row = zero_row
        for a in range(4):
            row = jnp.where(labels[a] == label, base + (q * 4 + a) * W, row)
        rows.append(pl.multiple_of(row, W))
    return rows


def intersect(qbuf, rows, partner):
    left = jnp.concatenate(
        [
            jnp.concatenate([qbuf[pl.ds(row, W), :] for row in rows_q], axis=1)
            for rows_q in rows
        ],
        axis=0,
    )
    return jnp.dot(left, partner, preferred_element_type=F32).astype(BF16)


def weighted(inter, amps, w0, w1):
    half = jnp.dot(inter, amps, preferred_element_type=F32)
    return (half[:W] * w0).astype(BF16), (half[W:] * w1).astype(BF16)


def frame(halves, inters):
    return lax.dot_general(
        jnp.concatenate(halves, axis=1),
        jnp.concatenate(inters, axis=1),
        (((1,), (1,)), ((), ())),
        preferred_element_type=F32,
    )


def place_of(tab_ref):
    return [tab_ref[PLACE + k].astype(jnp.int32) for k in range(4)]


def slot_of(pos, chunk):
    step, mine = chunk
    _, y, z, c = pos
    zz = jnp.where(c == 0, z - step, z + step) & (N_Z - 1)
    lane = c if mine else 1 - c
    return (y * N_Z + zz) * N_CORE + lane


def owner_of(pos, i):
    _, y, z, c = pos
    yy = (y - (i & 3)) & (N_Y - 1)
    lane = jnp.where(i < 4, c, 1 - c)
    return (yy * N_Z + z) * N_CORE + lane


def halves_into(hbuf, at, i, tab_ref, found, amps, inter_of):
    for j, (slot, row) in enumerate(found):
        weights = [tab_ref[(i * 2 + q) * 16 + (slot & 15)] for q in range(2)]
        half = weighted(inter_of(j), amps(j, row), *weights)
        for q in range(2):
            hbuf[at, q, :, pl.ds(j * W, W)] = half[q]


def frames_into(outs, prev_ref, hbuf, at, i, inter_of, n):
    for q in range(2):
        total = frame([hbuf[at, q]], [inter_of(j, q) for j in range(n)])
        if prev_ref is not None:
            total = total + prev_ref[i, q]
        outs[0][i, q] = total
        if len(outs) == 2:
            outs[1][i & 3, q] = total.astype(BF16)


def pack_kernel(*refs):
    parts, out_ref, sems = refs[:8], refs[8], refs[9]
    copies = [
        pltpu.make_async_copy(
            parts[k].at[pl.ds(0, 2 * OROWS)],
            out_ref.at[pl.ds(k * 2 * OROWS, 2 * OROWS)],
            sems.at[k],
        )
        for k in range(8)
    ]
    for copy in copies:
        copy.start()
    out_ref[pl.ds(QROWS, W), :] = jnp.zeros((W, W), BF16)
    for copy in copies:
        copy.wait()


def pack(parts):
    return pl.pallas_call(
        pack_kernel,
        out_shape=jax.ShapeDtypeStruct((QROWS + W, W), BF16),
        in_specs=[ANY] * 8,
        out_specs=VMEM,
        scratch_shapes=[pltpu.SemaphoreType.DMA((8,))],
        compiler_params=PARAMS,
        cost_estimate=cost(1),
    )(*parts)


def wanted_rows(pos, tab_ref, chunks, i):
    found = []
    for chunk in chunks:
        slot = slot_of(pos, chunk)
        row = tab_ref[ROWS + i * 16 + (slot & 15)].astype(jnp.int32)
        found.append((slot, row))
    return found


def first_kernel(chunks, places, n_data, has_prev, n_out, group_of, *refs):
    n = len(chunks)
    tab_ref = refs[0]
    qbuf = refs[1]
    p_refs = refs[2 : 2 + n_data]
    rest = refs[2 + n_data :]
    prev_ref = rest[0] if has_prev else None
    rest = rest[1 if has_prev else 0 :]
    inter_ref, outs, (hbuf, ibuf) = rest[0], rest[1 : 1 + n_out], rest[1 + n_out :]
    pos = place_of(tab_ref)

    def intersections(i, at):
        base = pl.multiple_of(i * 2 * OROWS, 2 * OROWS)
        q_id = owner_of(pos, i) * 2
        for j, (slot, row) in enumerate(wanted_rows(pos, tab_ref, chunks, i)):
            p_id = slot * 2 + row
            rows = [block_rows(tab_ref, base, q_id + q, p_id, q, QROWS) for q in range(2)]
            inter = intersect(
                qbuf, rows, p_refs[places[j][0]][places[j][1] + row, pl.ds(0, OROWS), :]
            )
            ibuf[at, j] = inter
            inter_ref[i, j] = inter

    def halves(i, at):
        found = wanted_rows(pos, tab_ref, chunks, i)
        amps = lambda j, row: p_refs[places[j][0]][places[j][1] + row, pl.ds(OROWS, W), :]
        halves_into(hbuf, at, i, tab_ref, found, amps, lambda j: ibuf[at, j])

    def frames(i, at):
        inter_of = lambda j, q: ibuf[at, j, pl.ds(q * W, W), :]
        frames_into(outs, prev_ref, hbuf, at, i, inter_of, n)

    in_turn([intersections, halves, frames], 8, group_of, (2, 1, 0))


def in_turn(stages, count, group_of, order):
    depth, count = len(stages), count // group_of

    def tick(s, parity):
        for k in order:
            if isinstance(s, int) and not 0 <= s - k < count:
                continue
            for t in range(group_of):
                stages[k]((s - k) * group_of + t, (parity + k) % 2 * group_of + t)

    start = depth - 1 + (count - depth + 1) % 2
    for s in range(start):
        tick(s, s % 2)

    @pl.loop(0, (count - start) // 2)
    def _(pair):
        tick(start + 2 * pair, start % 2)
        tick(start + 2 * pair + 1, (start + 1) % 2)

    for s in range(count, count + depth - 1):
        tick(s, s % 2)


def out_shapes(last):
    if not last:
        return (jax.ShapeDtypeStruct((8, 2, W, W), F32),)
    return (jax.ShapeDtypeStruct((8, 2, W, W), F32), jax.ShapeDtypeStruct((4, 2, W, W), BF16))


def first_couple(table, packed, chunks, places, data, prev, last):
    n = len(chunks)
    group_of = GROUPS[n]
    shapes = out_shapes(last)
    kernel = functools.partial(
        first_kernel, chunks, places, len(data), prev is not None, len(shapes), group_of
    )
    return pl.pallas_call(
        kernel,
        out_shape=(jax.ShapeDtypeStruct((8, n, 2 * W, W), BF16),) + shapes,
        in_specs=[SMEM] + [VMEM] * (1 + len(data) + (prev is not None)),
        out_specs=(VMEM,) * (1 + len(shapes)),
        scratch_shapes=[
            pltpu.VMEM((2 * group_of, 2, W, n * W), BF16),
            pltpu.VMEM((2 * group_of, n, 2 * W, W), BF16),
        ],
        compiler_params=PARAMS,
        cost_estimate=cost(1 + 1.7 * n),
    )(table, packed, *data, *([prev] if prev is not None else []))


def next_kernel(chunks, inter_at, places, n_inter, n_amps, has_prev, n_out, group_of, *refs):
    n = len(chunks)
    tab_ref = refs[0]
    inter_refs = refs[1 : 1 + n_inter]
    amp_refs = refs[1 + n_inter : 1 + n_inter + n_amps]
    prev_ref = refs[1 + n_inter + n_amps] if has_prev else None
    outs, hbuf = refs[-1 - n_out : -1], refs[-1]
    pos = place_of(tab_ref)

    def halves(i, at):
        found = wanted_rows(pos, tab_ref, chunks, i)
        amps = lambda j, row: amp_refs[places[j][0]][places[j][1] + row]
        inter_of = lambda j: inter_refs[inter_at[j][0]][i, inter_at[j][1]]
        halves_into(hbuf, at, i, tab_ref, found, amps, inter_of)

    def frames(i, at):
        inter_of = lambda j, q: inter_refs[inter_at[j][0]][i, inter_at[j][1], pl.ds(q * W, W), :]
        frames_into(outs, prev_ref, hbuf, at, i, inter_of, n)

    in_turn([halves, frames], 8, group_of, (0, 1))


def next_couple(table, inters, chunks, inter_at, places, amps, prev, last):
    n = len(chunks)
    group_of = GROUPS[n]
    shapes = out_shapes(last)
    kernel = functools.partial(
        next_kernel,
        chunks,
        inter_at,
        places,
        len(inters),
        len(amps),
        prev is not None,
        len(shapes),
        group_of,
    )
    return pl.pallas_call(
        kernel,
        out_shape=shapes,
        in_specs=[SMEM] + [VMEM] * (len(inters) + len(amps) + (prev is not None)),
        out_specs=(VMEM,) * len(shapes),
        scratch_shapes=[pltpu.VMEM((2 * group_of, 2, W, n * W), BF16)],
        compiler_params=PARAMS,
        cost_estimate=cost(1 + n),
    )(table, *inters, *amps, *([prev] if prev is not None else []))


def cross_first_kernel(tab_ref, below_ref, above_ref, own_ref, inter_ref, out_ref, qbuf):
    qbuf[pl.ds(0, 2 * OROWS), :] = own_ref[pl.ds(0, 2 * OROWS), :]
    qbuf[pl.ds(2 * OROWS, W), :] = jnp.zeros((W, W), BF16)
    group, y, z, c = [tab_ref[k].astype(jnp.int32) for k in range(4)]
    place_here = (y * N_Z + z) * N_CORE + c
    q_id = (group * N_DEV + place_here) * 2
    halves, inters = [[], []], [[], []]
    for j in range(4):
        there = jnp.clip(group + (1 if j >= 2 else -1), 0, 3)
        p_id = (there * N_DEV + place_here) * 2 + j % 2
        rows = [block_rows(tab_ref, 0, q_id + q, p_id, q, 2 * OROWS, 16) for q in range(2)]
        near_ref = below_ref if j < 2 else above_ref
        inter = intersect(qbuf, rows, near_ref[j % 2, pl.ds(0, OROWS), :])
        inter_ref[j] = inter
        half = weighted(
            inter, near_ref[j % 2, pl.ds(OROWS, W), :], tab_ref[8 + j], tab_ref[12 + j]
        )
        for q in range(2):
            halves[q].append(half[q])
            inters[q].append(inter[q * W : (q + 1) * W])
    for q in range(2):
        out_ref[q] = frame(halves[q], inters[q])


def cross_first(table, below, above, own):
    return pl.pallas_call(
        cross_first_kernel,
        out_shape=(
            jax.ShapeDtypeStruct((4, 2 * W, W), BF16),
            jax.ShapeDtypeStruct((2, W, W), F32),
        ),
        in_specs=[SMEM] + [VMEM] * 3,
        out_specs=(VMEM, VMEM),
        scratch_shapes=[pltpu.VMEM((2 * OROWS + W, W), BF16)],
        compiler_params=PARAMS,
        cost_estimate=cost(2),
    )(table, below, above, own)


def cross_next_kernel(tab_ref, inter_ref, below_ref, above_ref, out_ref):
    halves, inters = [[], []], [[], []]
    for j in range(4):
        amps = (below_ref if j < 2 else above_ref)[j % 2]
        inter = inter_ref[j]
        half = weighted(inter, amps, tab_ref[8 + j], tab_ref[12 + j])
        for q in range(2):
            halves[q].append(half[q])
            inters[q].append(inter[q * W : (q + 1) * W])
    for q in range(2):
        out_ref[q] = frame(halves[q], inters[q])


def cross_next(table, inter, below, above):
    return pl.pallas_call(
        cross_next_kernel,
        out_shape=jax.ShapeDtypeStruct((2, W, W), F32),
        in_specs=[SMEM] + [VMEM] * 3,
        out_specs=VMEM,
        compiler_params=PARAMS,
        cost_estimate=cost(1),
    )(table, inter, below, above)


def gather_shares(mine, others):
    total = mine[:N_Y] + swap(others).astype(F32)
    shares = [send_back(total[j].astype(BF16), j) for j in range(1, N_Y)]
    return total[0] + (shares[0].astype(F32) + shares[1].astype(F32) + shares[2].astype(F32))


def send_back(x, j):
    return along_y(x, -j)


def on_device(
    orbitals,
    domains,
    partners,
    active,
    fock_terms,
    exchange_ints,
    pno_energies,
    occ_energies,
    amplitudes,
):
    group = lax.axis_index("grp")
    dev = lax.axis_index("dev")
    pos = jnp.stack([group, dev // (N_Z * N_CORE), dev // N_CORE % N_Z, dev % N_CORE])
    near_ids = ((group + jnp.array([-1, -1, 1, 1])) * N_DEV + dev) * 2 + jnp.array([0, 1, 0, 1])
    same = partners[:, None, COUP_IN:] == near_ids[None, :, None]
    cross_w = jnp.sum(jnp.where(same, fock_terms[:, None, COUP_IN:], 0.0), axis=2).reshape(8)

    mine = bundle(orbitals, amplitudes)
    other = swap(mine)
    ring_a, ring_b = [mine], [other]
    for k in range(4):
        ring_a.append(along_z(ring_a[-1], 1))
        if k < 3:
            ring_b.append(along_z(ring_b[-1], 1))
    mine_then, _ = lax.optimization_barrier((mine, other))
    turned_mine = turned(active, mine_then, fock_terms, partners)
    from_below, from_above = along_y(turned_mine, 1), along_y(turned_mine, 3)
    _, from_below, from_above = lax.optimization_barrier((ring_b[1], from_below, from_above))
    passed = jnp.where(pos[3] == 0, from_below, from_above)
    from_far = send(passed, lambda y, z, c: place(y + 1 if c == 0 else y - 1, z, c))
    _, from_far = lax.optimization_barrier((ring_b[2], from_far))
    turned_all = [turned_mine, from_below, from_far, from_above]
    turned_all = turned_all + [swap(x) for x in turned_all]
    mine_later, _ = lax.optimization_barrier((mine, ring_b[2]))
    below = lax.ppermute(mine_later, "grp", [(0, 1), (1, 2), (2, 3), (3, 0)])
    above = lax.ppermute(mine_later, "grp", [(1, 0), (2, 1), (3, 2), (0, 3)])

    words = jnp.stack([x[2 * OROWS :] for x in turned_all]).astype(F32)
    words = words[:, 0:2] + words[:, 2:4] + words[:, 4:6]
    column = pos[1] * 16
    weights = lax.dynamic_slice_in_dim(words, column, 16, 2)
    wanted = lax.dynamic_slice_in_dim(words[:, 0], COUP_IN + column, 16, 1)
    labels = domains.astype(F32)
    here = lax.dynamic_slice_in_dim(labels, group * N_DEV * 2, N_DEV * 2, 0)
    spot = jnp.concatenate([pos.astype(F32), jnp.zeros(4, F32)])
    table = jnp.concatenate([weights.reshape(-1), wanted.reshape(-1), spot, here.reshape(-1)])
    cross_table = jnp.concatenate([spot, cross_w, labels.reshape(-1)])
    packed = pack(turned_all)

    chunks_1 = [(0, True), (1, True), (1, False), (2, True), (2, False)]
    places_1 = [(0, 0), (1, 0), (2, 0), (3, 0), (4, 0)]
    chunks_2 = [(3, True), (3, False)]
    places_2 = [(0, 0), (1, 0)]
    chunks_3 = [(4, True)]

    first = functools.partial(first_couple, table, packed)
    data_1 = [mine, ring_a[1], ring_b[1], ring_a[2], ring_b[2]]
    inter_1, part = first(chunks_1, places_1, data_1, None, False)
    inter_cross, cross = cross_first(cross_table, below, above, turned_mine)
    inter_2, part = first(chunks_2, places_2, [ring_a[3], ring_b[3]], part, False)
    part, cross = lax.optimization_barrier((part, cross))
    inter_3, own, others = first(chunks_3, [(0, 0)], [ring_a[4]], part, True)

    denominator = pno_energies[:, :, None] + pno_energies[:, None, :] - occ_energies[:, None, None]
    integrals = exchange_ints.astype(F32)
    coupled = gather_shares(own, others) + cross
    residual = integrals + denominator * amplitudes - coupled
    current = amplitudes - residual / denominator

    sent = current.astype(BF16)
    both = jnp.concatenate([sent, swap(sent)], axis=0)
    steps = [along_z(both, 1), along_z(both, 2)]
    steps.append(along_z(jnp.concatenate([steps[0], steps[1][:2]], axis=0), 2))
    sent_later, _ = lax.optimization_barrier((sent, steps[1]))
    below = lax.ppermute(sent_later, "grp", [(0, 1), (1, 2), (2, 3), (3, 0)])
    above = lax.ppermute(sent_later, "grp", [(1, 0), (2, 1), (3, 2), (0, 3)])

    (part,) = next_couple(
        table,
        [inter_1],
        chunks_1,
        [(0, j) for j in range(5)],
        [(0, 0), (1, 0), (1, 2), (2, 0), (2, 2)],
        [sent, steps[0], steps[1]],
        None,
        False,
    )
    cross = cross_next(cross_table, inter_cross, below, above)
    part, cross = lax.optimization_barrier((part, cross))
    own, others = next_couple(
        table,
        [inter_2, inter_3],
        chunks_2 + chunks_3,
        [(0, 0), (0, 1), (1, 0)],
        [(0, 0), (0, 2), (0, 4)],
        [steps[2]],
        part,
        True,
    )
    coupled = gather_shares(own, others) + cross
    residual = integrals + denominator * current - coupled
    updated = current - residual / denominator
    return updated, residual


def solution(mesh):
    placed = (
        P(("grp", "dev"), None, None, None),
        P(),
        P(("grp", "dev"), None),
        P(("grp", "dev")),
        P(("grp", "dev"), None),
        P(("grp", "dev"), None, None),
        P(("grp", "dev"), None),
        P(("grp", "dev")),
        P(("grp", "dev"), None, None),
    )
    return jax.shard_map(
        on_device,
        mesh=mesh,
        in_specs=placed,
        out_specs=(P(("grp", "dev"), None, None), P(("grp", "dev"), None, None)),
        check_vma=False,
    )
```

```python
import functools

import jax
import jax.numpy as jnp
from jax import lax
from jax.experimental import pallas as pl
from jax.experimental.pallas import tpu as pltpu
from jax.sharding import PartitionSpec as P

N_Y, N_Z, N_CORE = 4, 8, 2
N_DEV = N_Y * N_Z * N_CORE
COUP_IN = 64
ROWS = 256
PLACE = ROWS + 128
LABELS = PLACE + 8
QROWS = 8 * 2 * 512
GROUPS = {1: 4, 2: 4, 3: 2, 4: 2, 5: 2}
W = 128
OROWS = 512
BF16 = jnp.bfloat16
F32 = jnp.float32
SMEM = pl.BlockSpec(memory_space=pltpu.SMEM)
VMEM = pl.BlockSpec(memory_space=pltpu.VMEM)
ANY = pl.BlockSpec(memory_space=pl.ANY)
PARAMS = pltpu.CompilerParams(vmem_limit_bytes=20 * 1024 * 1024)


def place(y, z, c):
    return ((y % N_Y) * N_Z + z % N_Z) * N_CORE + c


def routes(move):
    return [
        (place(y, z, c), move(y, z, c))
        for y in range(N_Y)
        for z in range(N_Z)
        for c in range(N_CORE)
    ]


def send(x, move):
    return lax.ppermute(x, "dev", routes(move))


def swap(x):
    return send(x, lambda y, z, c: place(y, z, 1 - c))


def along_z(x, k):
    return send(x, lambda y, z, c: place(y, z + k if c == 0 else z - k, c))


def along_y(x, k):
    return send(x, lambda y, z, c: place(y + k, z, c))


def cost(microseconds):
    return pl.CostEstimate(
        flops=int(microseconds * 1.15e9), bytes_accessed=1024, transcendentals=0
    )


def bundle_kernel(orb_ref, amp_ref, out_ref, amps, sems):
    copies = [pltpu.make_async_copy(amp_ref, amps, sems.at[4])]
    for q in range(2):
        for a in range(4):
            copies.append(
                pltpu.make_async_copy(
                    orb_ref.at[q, a], out_ref.at[q, pl.ds(a * W, W)], sems.at[q * 4 + a + 5]
                )
            )
    for copy in copies:
        copy.start()
    copies[0].wait()
    out_ref[:, pl.ds(OROWS, W), :] = amps[...].astype(BF16)
    for copy in copies[1:]:
        copy.wait()


def bundle(orbitals, amplitudes):
    far = pl.BlockSpec(memory_space=pltpu.HBM)
    return pl.pallas_call(
        bundle_kernel,
        out_shape=jax.ShapeDtypeStruct((2, OROWS + W, W), BF16),
        in_specs=[far, far],
        out_specs=VMEM,
        scratch_shapes=[pltpu.VMEM((2, W, W), F32), pltpu.SemaphoreType.DMA((13,))],
        compiler_params=PARAMS,
        cost_estimate=cost(1),
    )(orbitals, amplitudes)


def turned_kernel(active_ref, own_ref, fock_ref, partner_ref, out_ref, words):
    for q in range(2):
        for a in range(4):
            out_ref[pl.ds((q * 4 + a) * W, W), :] = own_ref[q, pl.ds(a * W, W), :].T
    words[...] = jnp.zeros((16, W), F32)
    slot = lax.broadcasted_iota(jnp.int32, (1, COUP_IN), 1)
    for q in range(2):
        fock = fock_ref[pl.ds(q, 1), pl.ds(0, COUP_IN)]
        fock = jnp.where(slot < active_ref[q], fock, 0.0)
        high = fock.astype(BF16).astype(F32)
        middle = (fock - high).astype(BF16).astype(F32)
        words[pl.ds(q, 1), pl.ds(0, COUP_IN)] = high
        words[pl.ds(2 + q, 1), pl.ds(0, COUP_IN)] = middle
        words[pl.ds(4 + q, 1), pl.ds(0, COUP_IN)] = fock - high - middle
        wanted = (partner_ref[pl.ds(q, 1), pl.ds(0, COUP_IN)] & 1).astype(F32)
        words[pl.ds(q, 1), pl.ds(COUP_IN, COUP_IN)] = wanted
    out_ref[pl.ds(2 * OROWS, 16), :] = words[...].astype(BF16)


def turned(active, own, fock_terms, partners):
    return pl.pallas_call(
        turned_kernel,
        out_shape=jax.ShapeDtypeStruct((2 * OROWS + 16, W), BF16),
        in_specs=[SMEM, VMEM, VMEM, VMEM],
        out_specs=VMEM,
        scratch_shapes=[pltpu.VMEM((16, W), F32)],
        compiler_params=PARAMS,
        cost_estimate=cost(1),
    )(active, own, fock_terms, partners)


def block_rows(tab_ref, base, q_id, p_id, q, zero_row, start=LABELS):
    labels = [tab_ref[start + q_id * 4 + a] for a in range(4)]
    rows = []
    for b in range(4):
        label = tab_ref[start + p_id * 4 + b]
        row = zero_row
        for a in range(4):
            row = jnp.where(labels[a] == label, base + (q * 4 + a) * W, row)
        rows.append(pl.multiple_of(row, W))
    return rows


def intersect(qbuf, rows, partner):
    left = jnp.concatenate(
        [
            jnp.concatenate([qbuf[pl.ds(row, W), :] for row in rows_q], axis=1)
            for rows_q in rows
        ],
        axis=0,
    )
    return jnp.dot(left, partner, preferred_element_type=F32).astype(BF16)


def weighted(inter, amps, w0, w1):
    half = jnp.dot(inter, amps, preferred_element_type=F32)
    return (half[:W] * w0).astype(BF16), (half[W:] * w1).astype(BF16)


def frame(halves, inters):
    return lax.dot_general(
        jnp.concatenate(halves, axis=1),
        jnp.concatenate(inters, axis=1),
        (((1,), (1,)), ((), ())),
        preferred_element_type=F32,
    )


def place_of(tab_ref):
    return [tab_ref[PLACE + k].astype(jnp.int32) for k in range(4)]


def slot_of(pos, chunk):
    step, mine = chunk
    _, y, z, c = pos
    zz = jnp.where(c == 0, z - step, z + step) & (N_Z - 1)
    lane = c if mine else 1 - c
    return (y * N_Z + zz) * N_CORE + lane


def owner_of(pos, i):
    _, y, z, c = pos
    yy = (y - (i & 3)) & (N_Y - 1)
    lane = jnp.where(i < 4, c, 1 - c)
    return (yy * N_Z + z) * N_CORE + lane


def halves_into(hbuf, at, i, tab_ref, found, amps, inter_of):
    for j, (slot, row) in enumerate(found):
        weights = [tab_ref[(i * 2 + q) * 16 + (slot & 15)] for q in range(2)]
        half = weighted(inter_of(j), amps(j, row), *weights)
        for q in range(2):
            hbuf[at, q, :, pl.ds(j * W, W)] = half[q]


def frames_into(outs, prev_ref, hbuf, at, i, inter_of, n):
    for q in range(2):
        total = frame([hbuf[at, q]], [inter_of(j, q) for j in range(n)])
        if prev_ref is not None:
            total = total + prev_ref[i, q]
        outs[0][i, q] = total
        if len(outs) == 2:
            outs[1][i & 3, q] = total.astype(BF16)


def pack_kernel(*refs):
    parts, out_ref, sems = refs[:8], refs[8], refs[9]
    copies = [
        pltpu.make_async_copy(
            parts[k].at[pl.ds(0, 2 * OROWS)],
            out_ref.at[pl.ds(k * 2 * OROWS, 2 * OROWS)],
            sems.at[k],
        )
        for k in range(8)
    ]
    for copy in copies:
        copy.start()
    out_ref[pl.ds(QROWS, W), :] = jnp.zeros((W, W), BF16)
    for copy in copies:
        copy.wait()


def pack(parts):
    return pl.pallas_call(
        pack_kernel,
        out_shape=jax.ShapeDtypeStruct((QROWS + W, W), BF16),
        in_specs=[ANY] * 8,
        out_specs=VMEM,
        scratch_shapes=[pltpu.SemaphoreType.DMA((8,))],
        compiler_params=PARAMS,
        cost_estimate=cost(1),
    )(*parts)


def wanted_rows(pos, tab_ref, chunks, i):
    found = []
    for chunk in chunks:
        slot = slot_of(pos, chunk)
        row = tab_ref[ROWS + i * 16 + (slot & 15)].astype(jnp.int32)
        found.append((slot, row))
    return found


def first_kernel(chunks, places, n_data, has_prev, n_out, group_of, *refs):
    n = len(chunks)
    tab_ref = refs[0]
    qbuf = refs[1]
    p_refs = refs[2 : 2 + n_data]
    rest = refs[2 + n_data :]
    prev_ref = rest[0] if has_prev else None
    rest = rest[1 if has_prev else 0 :]
    inter_ref, outs, (hbuf, ibuf) = rest[0], rest[1 : 1 + n_out], rest[1 + n_out :]
    pos = place_of(tab_ref)

    def intersections(i, at):
        base = pl.multiple_of(i * 2 * OROWS, 2 * OROWS)
        q_id = owner_of(pos, i) * 2
        for j, (slot, row) in enumerate(wanted_rows(pos, tab_ref, chunks, i)):
            p_id = slot * 2 + row
            rows = [block_rows(tab_ref, base, q_id + q, p_id, q, QROWS) for q in range(2)]
            inter = intersect(
                qbuf, rows, p_refs[places[j][0]][places[j][1] + row, pl.ds(0, OROWS), :]
            )
            ibuf[at, j] = inter
            inter_ref[i, j] = inter

    def halves(i, at):
        found = wanted_rows(pos, tab_ref, chunks, i)
        amps = lambda j, row: p_refs[places[j][0]][places[j][1] + row, pl.ds(OROWS, W), :]
        halves_into(hbuf, at, i, tab_ref, found, amps, lambda j: ibuf[at, j])

    def frames(i, at):
        inter_of = lambda j, q: ibuf[at, j, pl.ds(q * W, W), :]
        frames_into(outs, prev_ref, hbuf, at, i, inter_of, n)

    in_turn([intersections, halves, frames], 8, group_of, (2, 1, 0))


def in_turn(stages, count, group_of, order):
    depth, count = len(stages), count // group_of

    def tick(s, parity):
        for k in order:
            if isinstance(s, int) and not 0 <= s - k < count:
                continue
            for t in range(group_of):
                stages[k]((s - k) * group_of + t, (parity + k) % 2 * group_of + t)

    start = depth - 1 + (count - depth + 1) % 2
    for s in range(start):
        tick(s, s % 2)

    @pl.loop(0, (count - start) // 2)
    def _(pair):
        tick(start + 2 * pair, start % 2)
        tick(start + 2 * pair + 1, (start + 1) % 2)

    for s in range(count, count + depth - 1):
        tick(s, s % 2)


def out_shapes(last):
    if not last:
        return (jax.ShapeDtypeStruct((8, 2, W, W), F32),)
    return (jax.ShapeDtypeStruct((8, 2, W, W), F32), jax.ShapeDtypeStruct((4, 2, W, W), BF16))


def first_couple(table, packed, chunks, places, data, prev, last):
    n = len(chunks)
    group_of = GROUPS[n]
    shapes = out_shapes(last)
    kernel = functools.partial(
        first_kernel, chunks, places, len(data), prev is not None, len(shapes), group_of
    )
    return pl.pallas_call(
        kernel,
        out_shape=(jax.ShapeDtypeStruct((8, n, 2 * W, W), BF16),) + shapes,
        in_specs=[SMEM] + [VMEM] * (1 + len(data) + (prev is not None)),
        out_specs=(VMEM,) * (1 + len(shapes)),
        scratch_shapes=[
            pltpu.VMEM((2 * group_of, 2, W, n * W), BF16),
            pltpu.VMEM((2 * group_of, n, 2 * W, W), BF16),
        ],
        compiler_params=PARAMS,
        cost_estimate=cost(0.8 + 0.96 * n),
    )(table, packed, *data, *([prev] if prev is not None else []))


def next_kernel(chunks, inter_at, places, n_inter, n_amps, has_prev, n_out, group_of, *refs):
    n = len(chunks)
    tab_ref = refs[0]
    inter_refs = refs[1 : 1 + n_inter]
    amp_refs = refs[1 + n_inter : 1 + n_inter + n_amps]
    prev_ref = refs[1 + n_inter + n_amps] if has_prev else None
    outs, hbuf = refs[-1 - n_out : -1], refs[-1]
    pos = place_of(tab_ref)

    def halves(i, at):
        found = wanted_rows(pos, tab_ref, chunks, i)
        amps = lambda j, row: amp_refs[places[j][0]][places[j][1] + row]
        inter_of = lambda j: inter_refs[inter_at[j][0]][i, inter_at[j][1]]
        halves_into(hbuf, at, i, tab_ref, found, amps, inter_of)

    def frames(i, at):
        inter_of = lambda j, q: inter_refs[inter_at[j][0]][i, inter_at[j][1], pl.ds(q * W, W), :]
        frames_into(outs, prev_ref, hbuf, at, i, inter_of, n)

    in_turn([halves, frames], 8, group_of, (0, 1))


def next_couple(table, inters, chunks, inter_at, places, amps, prev, last):
    n = len(chunks)
    group_of = GROUPS[n]
    shapes = out_shapes(last)
    kernel = functools.partial(
        next_kernel,
        chunks,
        inter_at,
        places,
        len(inters),
        len(amps),
        prev is not None,
        len(shapes),
        group_of,
    )
    return pl.pallas_call(
        kernel,
        out_shape=shapes,
        in_specs=[SMEM] + [VMEM] * (len(inters) + len(amps) + (prev is not None)),
        out_specs=(VMEM,) * len(shapes),
        scratch_shapes=[pltpu.VMEM((2 * group_of, 2, W, n * W), BF16)],
        compiler_params=PARAMS,
        cost_estimate=cost(0.4 + 0.4 * n),
    )(table, *inters, *amps, *([prev] if prev is not None else []))


def cross_first_kernel(tab_ref, below_ref, above_ref, own_ref, inter_ref, out_ref, qbuf):
    qbuf[pl.ds(0, 2 * OROWS), :] = own_ref[pl.ds(0, 2 * OROWS), :]
    qbuf[pl.ds(2 * OROWS, W), :] = jnp.zeros((W, W), BF16)
    group, y, z, c = [tab_ref[k].astype(jnp.int32) for k in range(4)]
    place_here = (y * N_Z + z) * N_CORE + c
    q_id = (group * N_DEV + place_here) * 2
    halves, inters = [[], []], [[], []]
    for j in range(4):
        there = jnp.clip(group + (1 if j >= 2 else -1), 0, 3)
        p_id = (there * N_DEV + place_here) * 2 + j % 2
        rows = [block_rows(tab_ref, 0, q_id + q, p_id, q, 2 * OROWS, 16) for q in range(2)]
        near_ref = below_ref if j < 2 else above_ref
        inter = intersect(qbuf, rows, near_ref[j % 2, pl.ds(0, OROWS), :])
        inter_ref[j] = inter
        half = weighted(
            inter, near_ref[j % 2, pl.ds(OROWS, W), :], tab_ref[8 + j], tab_ref[12 + j]
        )
        for q in range(2):
            halves[q].append(half[q])
            inters[q].append(inter[q * W : (q + 1) * W])
    for q in range(2):
        out_ref[q] = frame(halves[q], inters[q])


def cross_first(table, below, above, own):
    return pl.pallas_call(
        cross_first_kernel,
        out_shape=(
            jax.ShapeDtypeStruct((4, 2 * W, W), BF16),
            jax.ShapeDtypeStruct((2, W, W), F32),
        ),
        in_specs=[SMEM] + [VMEM] * 3,
        out_specs=(VMEM, VMEM),
        scratch_shapes=[pltpu.VMEM((2 * OROWS + W, W), BF16)],
        compiler_params=PARAMS,
        cost_estimate=cost(2),
    )(table, below, above, own)


def cross_next_kernel(tab_ref, inter_ref, below_ref, above_ref, out_ref):
    halves, inters = [[], []], [[], []]
    for j in range(4):
        amps = (below_ref if j < 2 else above_ref)[j % 2]
        inter = inter_ref[j]
        half = weighted(inter, amps, tab_ref[8 + j], tab_ref[12 + j])
        for q in range(2):
            halves[q].append(half[q])
            inters[q].append(inter[q * W : (q + 1) * W])
    for q in range(2):
        out_ref[q] = frame(halves[q], inters[q])


def cross_next(table, inter, below, above):
    return pl.pallas_call(
        cross_next_kernel,
        out_shape=jax.ShapeDtypeStruct((2, W, W), F32),
        in_specs=[SMEM] + [VMEM] * 3,
        out_specs=VMEM,
        compiler_params=PARAMS,
        cost_estimate=cost(1),
    )(table, inter, below, above)


def gather_shares(mine, others):
    total = mine[:N_Y] + swap(others).astype(F32)
    shares = [send_back(total[j].astype(BF16), j) for j in (2, 1, 3)]
    return total[0] + (shares[0].astype(F32) + shares[1].astype(F32) + shares[2].astype(F32))


def send_back(x, j):
    return along_y(x, -j)


def on_device(
    orbitals,
    domains,
    partners,
    active,
    fock_terms,
    exchange_ints,
    pno_energies,
    occ_energies,
    amplitudes,
):
    group = lax.axis_index("grp")
    dev = lax.axis_index("dev")
    pos = jnp.stack([group, dev // (N_Z * N_CORE), dev // N_CORE % N_Z, dev % N_CORE])
    near_ids = ((group + jnp.array([-1, -1, 1, 1])) * N_DEV + dev) * 2 + jnp.array([0, 1, 0, 1])
    same = partners[:, None, COUP_IN:] == near_ids[None, :, None]
    cross_w = jnp.sum(jnp.where(same, fock_terms[:, None, COUP_IN:], 0.0), axis=2).reshape(8)

    mine = bundle(orbitals, amplitudes)
    other = swap(mine)
    ring_a, ring_b = [mine], [other]
    for _ in range(3):
        ring_a.append(along_z(ring_a[-1], 1))
        ring_b.append(along_z(ring_b[-1], 1))
    mine_then, _ = lax.optimization_barrier((mine, other))
    turned_mine = turned(active, mine_then, fock_terms, partners)
    from_below, from_above = along_y(turned_mine, 1), along_y(turned_mine, 3)
    _, from_below, from_above = lax.optimization_barrier((ring_b[1], from_below, from_above))
    passed = jnp.where(pos[3] == 0, from_below, from_above)
    from_far = send(passed, lambda y, z, c: place(y + 1 if c == 0 else y - 1, z, c))
    below = lax.ppermute(mine, "grp", [(0, 1), (1, 2), (2, 3), (3, 0)])
    above = lax.ppermute(mine, "grp", [(1, 0), (2, 1), (3, 2), (0, 3)])
    _, below, above, from_far = lax.optimization_barrier((ring_b[2], below, above, from_far))
    turned_all = [turned_mine, from_below, from_far, from_above]
    turned_all = turned_all + [swap(x) for x in turned_all]

    words = jnp.stack([x[2 * OROWS :] for x in turned_all]).astype(F32)
    words = words[:, 0:2] + words[:, 2:4] + words[:, 4:6]
    column = pos[1] * 16
    weights = lax.dynamic_slice_in_dim(words, column, 16, 2)
    wanted = lax.dynamic_slice_in_dim(words[:, 0], COUP_IN + column, 16, 1)
    labels = domains.astype(F32)
    here = lax.dynamic_slice_in_dim(labels, group * N_DEV * 2, N_DEV * 2, 0)
    spot = jnp.concatenate([pos.astype(F32), jnp.zeros(4, F32)])
    table = jnp.concatenate([weights.reshape(-1), wanted.reshape(-1), spot, here.reshape(-1)])
    cross_table = jnp.concatenate([spot, cross_w, labels.reshape(-1)])
    packed = pack(turned_all)

    chunks_1 = [(0, True), (1, True), (1, False), (2, True), (2, False)]
    places_1 = [(0, 0), (1, 0), (2, 0), (3, 0), (4, 0)]
    chunks_2 = [(3, True), (3, False)]
    places_2 = [(0, 0), (1, 0)]
    chunks_3 = [(4, True)]

    first = functools.partial(first_couple, table, packed)
    data_1 = [mine, ring_a[1], ring_b[1], ring_a[2], ring_b[2]]
    inter_1, part = first(chunks_1, places_1, data_1, None, False)
    last_hop, part = lax.optimization_barrier((ring_a[3], part))
    ring_a.append(along_z(last_hop, 1))
    inter_2, part = first(chunks_2, places_2, [ring_a[3], ring_b[3]], part, False)
    inter_cross, cross = cross_first(cross_table, below, above, turned_mine)
    part, cross = lax.optimization_barrier((part, cross))
    inter_3, own, others = first(chunks_3, [(0, 0)], [ring_a[4]], part, True)

    denominator = pno_energies[:, :, None] + pno_energies[:, None, :] - occ_energies[:, None, None]
    integrals = exchange_ints.astype(F32)
    coupled = gather_shares(own, others) + cross
    residual = integrals + denominator * amplitudes - coupled
    current = amplitudes - residual / denominator

    sent = current.astype(BF16)
    both = jnp.concatenate([sent, swap(sent)], axis=0)
    third, second, first_step = [along_z(both, k) for k in (3, 2, 1)]
    steps = [first_step, second, third]
    far = along_z(third[:2], 1)

    (part,) = next_couple(
        table,
        [inter_1],
        chunks_1,
        [(0, j) for j in range(5)],
        [(0, 0), (1, 0), (1, 2), (2, 0), (2, 2)],
        [sent, steps[0], steps[1]],
        None,
        False,
    )
    near, _ = lax.optimization_barrier((sent, third))
    below = lax.ppermute(near, "grp", [(0, 1), (1, 2), (2, 3), (3, 0)])
    above = lax.ppermute(near, "grp", [(1, 0), (2, 1), (3, 2), (0, 3)])
    part, below, above = lax.optimization_barrier((part, below, above))
    cross = cross_next(cross_table, inter_cross, below, above)
    own, others = next_couple(
        table,
        [inter_2, inter_3],
        chunks_2 + chunks_3,
        [(0, 0), (0, 1), (1, 0)],
        [(0, 0), (0, 2), (1, 0)],
        [steps[2], far],
        part,
        True,
    )
    coupled = gather_shares(own, others) + cross
    residual = integrals + denominator * current - coupled
    updated = current - residual / denominator
    return updated, residual


def solution(mesh):
    placed = (
        P(("grp", "dev"), None, None, None),
        P(),
        P(("grp", "dev"), None),
        P(("grp", "dev")),
        P(("grp", "dev"), None),
        P(("grp", "dev"), None, None),
        P(("grp", "dev"), None),
        P(("grp", "dev")),
        P(("grp", "dev"), None, None),
    )
    return jax.shard_map(
        on_device,
        mesh=mesh,
        in_specs=placed,
        out_specs=(P(("grp", "dev"), None, None), P(("grp", "dev"), None, None)),
        check_vma=False,
    )
```

```python
import functools

import jax
import jax.numpy as jnp
from jax import lax
from jax.experimental import pallas as pl
from jax.experimental.pallas import tpu as pltpu
from jax.sharding import PartitionSpec as P

N_Y, N_Z, N_CORE = 4, 8, 2
N_DEV = N_Y * N_Z * N_CORE
COUP_IN = 64
ROWS = 256
PLACE = ROWS + 128
LABELS = PLACE + 8
QROWS = 8 * 2 * 512
GROUPS = {1: 4, 2: 4, 3: 2, 4: 2, 5: 2}
W = 128
OROWS = 512
BF16 = jnp.bfloat16
F32 = jnp.float32
SMEM = pl.BlockSpec(memory_space=pltpu.SMEM)
VMEM = pl.BlockSpec(memory_space=pltpu.VMEM)
ANY = pl.BlockSpec(memory_space=pl.ANY)
PARAMS = pltpu.CompilerParams(vmem_limit_bytes=20 * 1024 * 1024)


def place(y, z, c):
    return ((y % N_Y) * N_Z + z % N_Z) * N_CORE + c


def routes(move):
    return [
        (place(y, z, c), move(y, z, c))
        for y in range(N_Y)
        for z in range(N_Z)
        for c in range(N_CORE)
    ]


def send(x, move):
    return lax.ppermute(x, "dev", routes(move))


def swap(x):
    return send(x, lambda y, z, c: place(y, z, 1 - c))


def along_z(x, k):
    return send(x, lambda y, z, c: place(y, z + k if c == 0 else z - k, c))


def along_y(x, k):
    return send(x, lambda y, z, c: place(y + k, z, c))


def cost(microseconds):
    return pl.CostEstimate(
        flops=int(microseconds * 1.15e9), bytes_accessed=1024, transcendentals=0
    )


def bundle_kernel(orb_ref, amp_ref, out_ref, amps, sems):
    copies = [pltpu.make_async_copy(amp_ref, amps, sems.at[4])]
    for q in range(2):
        for a in range(4):
            copies.append(
                pltpu.make_async_copy(
                    orb_ref.at[q, a], out_ref.at[q, pl.ds(a * W, W)], sems.at[q * 4 + a + 5]
                )
            )
    for copy in copies:
        copy.start()
    copies[0].wait()
    out_ref[:, pl.ds(OROWS, W), :] = amps[...].astype(BF16)
    for copy in copies[1:]:
        copy.wait()


def bundle(orbitals, amplitudes):
    far = pl.BlockSpec(memory_space=pltpu.HBM)
    return pl.pallas_call(
        bundle_kernel,
        out_shape=jax.ShapeDtypeStruct((2, OROWS + W, W), BF16),
        in_specs=[far, far],
        out_specs=VMEM,
        scratch_shapes=[pltpu.VMEM((2, W, W), F32), pltpu.SemaphoreType.DMA((13,))],
        compiler_params=PARAMS,
        cost_estimate=cost(1),
    )(orbitals, amplitudes)


def turned_kernel(active_ref, own_ref, fock_ref, partner_ref, out_ref, words):
    for q in range(2):
        for a in range(4):
            out_ref[pl.ds((q * 4 + a) * W, W), :] = own_ref[q, pl.ds(a * W, W), :].T
    words[...] = jnp.zeros((16, W), F32)
    slot = lax.broadcasted_iota(jnp.int32, (1, COUP_IN), 1)
    for q in range(2):
        fock = fock_ref[pl.ds(q, 1), pl.ds(0, COUP_IN)]
        fock = jnp.where(slot < active_ref[q], fock, 0.0)
        high = fock.astype(BF16).astype(F32)
        middle = (fock - high).astype(BF16).astype(F32)
        words[pl.ds(q, 1), pl.ds(0, COUP_IN)] = high
        words[pl.ds(2 + q, 1), pl.ds(0, COUP_IN)] = middle
        words[pl.ds(4 + q, 1), pl.ds(0, COUP_IN)] = fock - high - middle
        wanted = (partner_ref[pl.ds(q, 1), pl.ds(0, COUP_IN)] & 1).astype(F32)
        words[pl.ds(q, 1), pl.ds(COUP_IN, COUP_IN)] = wanted
    out_ref[pl.ds(2 * OROWS, 16), :] = words[...].astype(BF16)


def turned(active, own, fock_terms, partners):
    return pl.pallas_call(
        turned_kernel,
        out_shape=jax.ShapeDtypeStruct((2 * OROWS + 16, W), BF16),
        in_specs=[SMEM, VMEM, VMEM, VMEM],
        out_specs=VMEM,
        scratch_shapes=[pltpu.VMEM((16, W), F32)],
        compiler_params=PARAMS,
        cost_estimate=cost(1),
    )(active, own, fock_terms, partners)


def block_rows(tab_ref, base, q_id, p_id, q, zero_row, start=LABELS):
    labels = [tab_ref[start + q_id * 4 + a] for a in range(4)]
    rows = []
    for b in range(4):
        label = tab_ref[start + p_id * 4 + b]
        row = zero_row
        for a in range(4):
            row = jnp.where(labels[a] == label, base + (q * 4 + a) * W, row)
        rows.append(pl.multiple_of(row, W))
    return rows


def intersect(qbuf, rows, partner):
    left = jnp.concatenate(
        [
            jnp.concatenate([qbuf[pl.ds(row, W), :] for row in rows_q], axis=1)
            for rows_q in rows
        ],
        axis=0,
    )
    return jnp.dot(left, partner, preferred_element_type=F32).astype(BF16)


def weighted(inter, amps, w0, w1):
    half = jnp.dot(inter, amps, preferred_element_type=F32)
    return (half[:W] * w0).astype(BF16), (half[W:] * w1).astype(BF16)


def frame(halves, inters):
    return lax.dot_general(
        jnp.concatenate(halves, axis=1),
        jnp.concatenate(inters, axis=1),
        (((1,), (1,)), ((), ())),
        preferred_element_type=F32,
    )


def place_of(tab_ref):
    return [tab_ref[PLACE + k].astype(jnp.int32) for k in range(4)]


def slot_of(pos, chunk):
    step, mine = chunk
    _, y, z, c = pos
    zz = jnp.where(c == 0, z - step, z + step) & (N_Z - 1)
    lane = c if mine else 1 - c
    return (y * N_Z + zz) * N_CORE + lane


def owner_of(pos, i):
    _, y, z, c = pos
    yy = (y - (i & 3)) & (N_Y - 1)
    lane = jnp.where(i < 4, c, 1 - c)
    return (yy * N_Z + z) * N_CORE + lane


def halves_into(hbuf, at, i, tab_ref, found, amps, inter_of):
    for j, (slot, row) in enumerate(found):
        weights = [tab_ref[(i * 2 + q) * 16 + (slot & 15)] for q in range(2)]
        half = weighted(inter_of(j), amps(j, row), *weights)
        for q in range(2):
            hbuf[at, q, :, pl.ds(j * W, W)] = half[q]


def frames_into(out_ref, prev_ref, hbuf, at, i, t, inter_of, n):
    for q in range(2):
        total = frame([hbuf[at, q]], [inter_of(j, q) for j in range(n)])
        if prev_ref is not None:
            total = total + prev_ref[i, q]
        out_ref[t, q] = total.astype(out_ref.dtype)


def pack_kernel(*refs):
    parts, out_ref, sems = refs[:8], refs[8], refs[9]
    copies = [
        pltpu.make_async_copy(
            parts[k].at[pl.ds(0, 2 * OROWS)],
            out_ref.at[pl.ds(k * 2 * OROWS, 2 * OROWS)],
            sems.at[k],
        )
        for k in range(8)
    ]
    for copy in copies:
        copy.start()
    out_ref[pl.ds(QROWS, W), :] = jnp.zeros((W, W), BF16)
    for copy in copies:
        copy.wait()


def pack(parts):
    return pl.pallas_call(
        pack_kernel,
        out_shape=jax.ShapeDtypeStruct((QROWS + W, W), BF16),
        in_specs=[ANY] * 8,
        out_specs=VMEM,
        scratch_shapes=[pltpu.SemaphoreType.DMA((8,))],
        compiler_params=PARAMS,
        cost_estimate=cost(1),
    )(*parts)


def wanted_rows(pos, tab_ref, chunks, i):
    found = []
    for chunk in chunks:
        slot = slot_of(pos, chunk)
        row = tab_ref[ROWS + i * 16 + (slot & 15)].astype(jnp.int32)
        found.append((slot, row))
    return found


def first_kernel(chunks, places, n_data, has_prev, span, group_of, *refs):
    n = len(chunks)
    tab_ref = refs[0]
    qbuf = refs[1]
    p_refs = refs[2 : 2 + n_data]
    rest = refs[2 + n_data :]
    prev_ref = rest[0] if has_prev else None
    rest = rest[1 if has_prev else 0 :]
    inter_ref, out_ref, hbuf, ibuf = rest
    begin, count = span
    pos = place_of(tab_ref)

    def intersections(t, at):
        i = t + begin
        base = pl.multiple_of(i * 2 * OROWS, 2 * OROWS)
        q_id = owner_of(pos, i) * 2
        for j, (slot, row) in enumerate(wanted_rows(pos, tab_ref, chunks, i)):
            p_id = slot * 2 + row
            rows = [block_rows(tab_ref, base, q_id + q, p_id, q, QROWS) for q in range(2)]
            inter = intersect(
                qbuf, rows, p_refs[places[j][0]][places[j][1] + row, pl.ds(0, OROWS), :]
            )
            ibuf[at, j] = inter
            inter_ref[t, j] = inter

    def halves(t, at):
        found = wanted_rows(pos, tab_ref, chunks, t + begin)
        amps = lambda j, row: p_refs[places[j][0]][places[j][1] + row, pl.ds(OROWS, W), :]
        halves_into(hbuf, at, t + begin, tab_ref, found, amps, lambda j: ibuf[at, j])

    def frames(t, at):
        inter_of = lambda j, q: ibuf[at, j, pl.ds(q * W, W), :]
        frames_into(out_ref, prev_ref, hbuf, at, t + begin, t, inter_of, n)

    in_turn([intersections, halves, frames], count, group_of, (2, 1, 0))


def in_turn(stages, count, group_of, order):
    depth, count = len(stages), count // group_of

    def tick(s, parity):
        for k in order:
            if isinstance(s, int) and not 0 <= s - k < count:
                continue
            for t in range(group_of):
                stages[k]((s - k) * group_of + t, (parity + k) % 2 * group_of + t)

    start = depth - 1 + (count - depth + 1) % 2
    for s in range(start):
        tick(s, s % 2)

    @pl.loop(0, (count - start) // 2)
    def _(pair):
        tick(start + 2 * pair, start % 2)
        tick(start + 2 * pair + 1, (start + 1) % 2)

    for s in range(count, count + depth - 1):
        tick(s, s % 2)


def first_couple(table, packed, chunks, places, data, prev, span=(0, 8), out_type=F32):
    n, count = len(chunks), span[1]
    group_of = min(GROUPS[n], count // 2)
    kernel = functools.partial(
        first_kernel, chunks, places, len(data), prev is not None, span, group_of
    )
    return pl.pallas_call(
        kernel,
        out_shape=(
            jax.ShapeDtypeStruct((count, n, 2 * W, W), BF16),
            jax.ShapeDtypeStruct((count, 2, W, W), out_type),
        ),
        in_specs=[SMEM] + [VMEM] * (1 + len(data) + (prev is not None)),
        out_specs=(VMEM, VMEM),
        scratch_shapes=[
            pltpu.VMEM((2 * group_of, 2, W, n * W), BF16),
            pltpu.VMEM((2 * group_of, n, 2 * W, W), BF16),
        ],
        compiler_params=PARAMS,
        cost_estimate=cost((0.8 + 0.96 * n) * (0.3 + 0.7 * count / 8)),
    )(table, packed, *data, *([prev] if prev is not None else []))


def next_kernel(chunks, inter_at, places, n_inter, n_amps, has_prev, span, group_of, *refs):
    n = len(chunks)
    begin, count = span
    tab_ref = refs[0]
    inter_refs = refs[1 : 1 + n_inter]
    amp_refs = refs[1 + n_inter : 1 + n_inter + n_amps]
    prev_ref = refs[1 + n_inter + n_amps] if has_prev else None
    out_ref, hbuf = refs[-2:]
    pos = place_of(tab_ref)

    def inter_row(j, t):
        ref = inter_refs[inter_at[j][0]]
        return ref.at[t + begin if ref.shape[0] == 8 else t, inter_at[j][1]]

    def halves(t, at):
        found = wanted_rows(pos, tab_ref, chunks, t + begin)
        amps = lambda j, row: amp_refs[places[j][0]][places[j][1] + row]
        halves_into(
            hbuf, at, t + begin, tab_ref, found, amps, lambda j: inter_row(j, t)[...]
        )

    def frames(t, at):
        inter_of = lambda j, q: inter_row(j, t)[pl.ds(q * W, W), :]
        frames_into(out_ref, prev_ref, hbuf, at, t + begin, t, inter_of, n)

    in_turn([halves, frames], count, group_of, (0, 1))


def next_couple(
    table, inters, chunks, inter_at, places, amps, prev, span=(0, 8), out_type=F32
):
    n, count = len(chunks), span[1]
    group_of = min(GROUPS[n], count // 2)
    kernel = functools.partial(
        next_kernel,
        chunks,
        inter_at,
        places,
        len(inters),
        len(amps),
        prev is not None,
        span,
        group_of,
    )
    return pl.pallas_call(
        kernel,
        out_shape=jax.ShapeDtypeStruct((count, 2, W, W), out_type),
        in_specs=[SMEM] + [VMEM] * (len(inters) + len(amps) + (prev is not None)),
        out_specs=VMEM,
        scratch_shapes=[pltpu.VMEM((2 * group_of, 2, W, n * W), BF16)],
        compiler_params=PARAMS,
        cost_estimate=cost((0.4 + 0.4 * n) * (0.3 + 0.7 * count / 8)),
    )(table, *inters, *amps, *([prev] if prev is not None else []))


def cross_first_kernel(tab_ref, below_ref, above_ref, own_ref, inter_ref, out_ref, qbuf):
    qbuf[pl.ds(0, 2 * OROWS), :] = own_ref[pl.ds(0, 2 * OROWS), :]
    qbuf[pl.ds(2 * OROWS, W), :] = jnp.zeros((W, W), BF16)
    group, y, z, c = [tab_ref[k].astype(jnp.int32) for k in range(4)]
    place_here = (y * N_Z + z) * N_CORE + c
    q_id = (group * N_DEV + place_here) * 2
    halves, inters = [[], []], [[], []]
    for j in range(4):
        there = jnp.clip(group + (1 if j >= 2 else -1), 0, 3)
        p_id = (there * N_DEV + place_here) * 2 + j % 2
        rows = [block_rows(tab_ref, 0, q_id + q, p_id, q, 2 * OROWS, 16) for q in range(2)]
        near_ref = below_ref if j < 2 else above_ref
        inter = intersect(qbuf, rows, near_ref[j % 2, pl.ds(0, OROWS), :])
        inter_ref[j] = inter
        half = weighted(
            inter, near_ref[j % 2, pl.ds(OROWS, W), :], tab_ref[8 + j], tab_ref[12 + j]
        )
        for q in range(2):
            halves[q].append(half[q])
            inters[q].append(inter[q * W : (q + 1) * W])
    for q in range(2):
        out_ref[q] = frame(halves[q], inters[q])


def cross_first(table, below, above, own):
    return pl.pallas_call(
        cross_first_kernel,
        out_shape=(
            jax.ShapeDtypeStruct((4, 2 * W, W), BF16),
            jax.ShapeDtypeStruct((2, W, W), F32),
        ),
        in_specs=[SMEM] + [VMEM] * 3,
        out_specs=(VMEM, VMEM),
        scratch_shapes=[pltpu.VMEM((2 * OROWS + W, W), BF16)],
        compiler_params=PARAMS,
        cost_estimate=cost(2),
    )(table, below, above, own)


def cross_next_kernel(tab_ref, inter_ref, below_ref, above_ref, out_ref):
    halves, inters = [[], []], [[], []]
    for j in range(4):
        amps = (below_ref if j < 2 else above_ref)[j % 2]
        inter = inter_ref[j]
        half = weighted(inter, amps, tab_ref[8 + j], tab_ref[12 + j])
        for q in range(2):
            halves[q].append(half[q])
            inters[q].append(inter[q * W : (q + 1) * W])
    for q in range(2):
        out_ref[q] = frame(halves[q], inters[q])


def cross_next(table, inter, below, above):
    return pl.pallas_call(
        cross_next_kernel,
        out_shape=jax.ShapeDtypeStruct((2, W, W), F32),
        in_specs=[SMEM] + [VMEM] * 3,
        out_specs=VMEM,
        compiler_params=PARAMS,
        cost_estimate=cost(1),
    )(table, inter, below, above)


def gather_shares(mine, others):
    total = mine[:N_Y] + swap(others).astype(F32)
    shares = [send_back(total[j].astype(BF16), j) for j in (2, 1, 3)]
    return total[0] + (shares[0].astype(F32) + shares[1].astype(F32) + shares[2].astype(F32))


def send_back(x, j):
    return along_y(x, -j)


def on_device(
    orbitals,
    domains,
    partners,
    active,
    fock_terms,
    exchange_ints,
    pno_energies,
    occ_energies,
    amplitudes,
):
    group = lax.axis_index("grp")
    dev = lax.axis_index("dev")
    pos = jnp.stack([group, dev // (N_Z * N_CORE), dev // N_CORE % N_Z, dev % N_CORE])
    near_ids = ((group + jnp.array([-1, -1, 1, 1])) * N_DEV + dev) * 2 + jnp.array([0, 1, 0, 1])
    same = partners[:, None, COUP_IN:] == near_ids[None, :, None]
    cross_w = jnp.sum(jnp.where(same, fock_terms[:, None, COUP_IN:], 0.0), axis=2).reshape(8)

    mine = bundle(orbitals, amplitudes)
    other = swap(mine)
    ring_a, ring_b = [mine], [other]
    for _ in range(3):
        ring_a.append(along_z(ring_a[-1], 1))
        ring_b.append(along_z(ring_b[-1], 1))
    mine_then, _ = lax.optimization_barrier((mine, other))
    turned_mine = turned(active, mine_then, fock_terms, partners)
    from_below, from_above = along_y(turned_mine, 1), along_y(turned_mine, 3)
    _, from_below, from_above = lax.optimization_barrier((ring_b[1], from_below, from_above))
    passed = jnp.where(pos[3] == 0, from_below, from_above)
    from_far = send(passed, lambda y, z, c: place(y + 1 if c == 0 else y - 1, z, c))
    below = lax.ppermute(mine, "grp", [(0, 1), (1, 2), (2, 3), (3, 0)])
    above = lax.ppermute(mine, "grp", [(1, 0), (2, 1), (3, 2), (0, 3)])
    _, below, above, from_far = lax.optimization_barrier((ring_b[2], below, above, from_far))
    turned_all = [turned_mine, from_below, from_far, from_above]
    turned_all = turned_all + [swap(x) for x in turned_all]

    words = jnp.stack([x[2 * OROWS :] for x in turned_all]).astype(F32)
    words = words[:, 0:2] + words[:, 2:4] + words[:, 4:6]
    column = pos[1] * 16
    weights = lax.dynamic_slice_in_dim(words, column, 16, 2)
    wanted = lax.dynamic_slice_in_dim(words[:, 0], COUP_IN + column, 16, 1)
    labels = domains.astype(F32)
    here = lax.dynamic_slice_in_dim(labels, group * N_DEV * 2, N_DEV * 2, 0)
    spot = jnp.concatenate([pos.astype(F32), jnp.zeros(4, F32)])
    table = jnp.concatenate([weights.reshape(-1), wanted.reshape(-1), spot, here.reshape(-1)])
    cross_table = jnp.concatenate([spot, cross_w, labels.reshape(-1)])
    packed = pack(turned_all)

    chunks_1 = [(0, True), (1, True), (1, False), (2, True), (2, False)]
    places_1 = [(0, 0), (1, 0), (2, 0), (3, 0), (4, 0)]
    chunks_2 = [(3, True), (3, False)]
    places_2 = [(0, 0), (1, 0)]
    chunks_3 = [(4, True)]

    first = functools.partial(first_couple, table, packed)
    data_1 = [mine, ring_a[1], ring_b[1], ring_a[2], ring_b[2]]
    inter_1, part = first(chunks_1, places_1, data_1, None)
    last_hop, part = lax.optimization_barrier((ring_a[3], part))
    ring_a.append(along_z(last_hop, 1))
    inter_2, part = first(chunks_2, places_2, [ring_a[3], ring_b[3]], part)
    inter_cross, cross = cross_first(cross_table, below, above, turned_mine)
    part, cross = lax.optimization_barrier((part, cross))
    last_part = functools.partial(first, chunks_3, [(0, 0)], [ring_a[4]], part)
    inter_other, others = last_part((4, 4), BF16)
    inter_own, own = last_part((0, 4), F32)

    denominator = pno_energies[:, :, None] + pno_energies[:, None, :] - occ_energies[:, None, None]
    integrals = exchange_ints.astype(F32)
    coupled = gather_shares(own, others) + cross
    residual = integrals + denominator * amplitudes - coupled
    current = amplitudes - residual / denominator

    sent = current.astype(BF16)
    both = jnp.concatenate([sent, swap(sent)], axis=0)
    third, second, first_step = [along_z(both, k) for k in (3, 2, 1)]
    steps = [first_step, second, third]
    far = along_z(third[:2], 1)

    part = next_couple(
        table,
        [inter_1],
        chunks_1,
        [(0, j) for j in range(5)],
        [(0, 0), (1, 0), (1, 2), (2, 0), (2, 2)],
        [sent, steps[0], steps[1]],
        None,
    )
    near, _ = lax.optimization_barrier((sent, third))
    below = lax.ppermute(near, "grp", [(0, 1), (1, 2), (2, 3), (3, 0)])
    above = lax.ppermute(near, "grp", [(1, 0), (2, 1), (3, 2), (0, 3)])
    part, below, above = lax.optimization_barrier((part, below, above))
    cross = cross_next(cross_table, inter_cross, below, above)
    late = [(0, 0), (0, 1), (1, 0)]
    late_amps = [(0, 0), (0, 2), (1, 0)]
    chunks_23 = chunks_2 + chunks_3
    amps_23 = [steps[2], far]
    others = next_couple(
        table, [inter_2, inter_other], chunks_23, late, late_amps, amps_23, part, (4, 4), BF16
    )
    own = next_couple(
        table, [inter_2, inter_own], chunks_23, late, late_amps, amps_23, part, (0, 4), F32
    )
    coupled = gather_shares(own, others) + cross
    residual = integrals + denominator * current - coupled
    updated = current - residual / denominator
    return updated, residual


def solution(mesh):
    placed = (
        P(("grp", "dev"), None, None, None),
        P(),
        P(("grp", "dev"), None),
        P(("grp", "dev")),
        P(("grp", "dev"), None),
        P(("grp", "dev"), None, None),
        P(("grp", "dev"), None),
        P(("grp", "dev")),
        P(("grp", "dev"), None, None),
    )
    return jax.shard_map(
        on_device,
        mesh=mesh,
        in_specs=placed,
        out_specs=(P(("grp", "dev"), None, None), P(("grp", "dev"), None, None)),
        check_vma=False,
    )
```
